32 devices in a mesh: grid: 8 (over z, y), slab: 4 (over x, core).
Axes of the slice: x: 2, y: 2, z: 4, core: 2. Of those that a mesh axis runs over, the one named last changes fastest.
Arguments:
- support: bfloat16 [64, 4, 32, 1024], P('grid', None, 'slab'), may hold values from -0.359375 to 0.359375
- potential: bfloat16 [256, 512], P(('grid', 'slab')), may hold values from -6 to 6
- kernel: float32 [64, 4, 4], P('grid'), may hold values from -18 to 18
- block_list: int32 [64, 4, 16], P('grid', 'slab'), may hold values from 0 to 255, as said below
Outputs:
- applied: bfloat16 [64, 4, 32, 1024], P('grid', None, 'slab')
- density: float32 [256, 512], P(('grid', 'slab'))
- hamiltonian: float32 [64, 4, 4], P('grid')
The draws below stay inside these ranges and needn't reach their ends.
Inputs may be any that keep to these rules, and one draw needn't show every extreme that they name: (block_list[a, l, j] // 8) % 4 == l. Within one layer, the 8 atoms of one grid index name blocks with any one value of block // 32 at most 32 times, and exactly 32 times for some value.
All inputs are finite; a program needn't handle non-finite values.
Results may differ from the reference program's by a relative error of at most 0.0004.
Values may be sent and summed in bfloat16 or wider, within the bound.
A program may use at most 64 MiB of HBM per device.

```python
import jax
import jax.numpy as jnp
from jax import lax

ATOM_DEV = 8
BLK_DEV = 8
FUNCS = 4
BOX = 32
BLOCK = 8
RADIUS = 13
LAYERS = 4
SIDE_BLOCKS = 4
SLOTS = 16
ATOMS = 64
BLOCKS = 256
N_GRID = 8


def draw_block_list(key, part):
    requests = ATOM_DEV * SLOTS
    capacity = max(2, 2 * requests // N_GRID)
    remainder = requests - capacity

    def sender(index_value):
        sender_key = jax.random.fold_in(key, index_value)
        first_key, second_key, third_key, fourth_key = jax.random.split(sender_key, 4)
        layer_index = index_value % LAYERS
        busiest = jax.random.randint(first_key, (), 0, N_GRID, dtype=jnp.int32)
        others = (busiest + 1 + jnp.arange((N_GRID - 1) * capacity, dtype=jnp.int32) // capacity) % N_GRID
        others = jax.random.permutation(second_key, others)[:remainder]
        peer_list = jnp.concatenate([jnp.full((capacity,), busiest, jnp.int32), others])
        peer_list = jax.random.permutation(third_key, peer_list)
        local_block = jax.random.randint(fourth_key, (requests,), 0, BLK_DEV, dtype=jnp.int32)
        return ((peer_list * LAYERS + layer_index) * BLK_DEV + local_block).reshape(ATOM_DEV, SLOTS)
    drawn_lists = jax.vmap(sender)(jnp.arange(N_GRID * LAYERS, dtype=jnp.int32))
    drawn_lists = drawn_lists.reshape(N_GRID, LAYERS, ATOM_DEV, SLOTS)
    return jnp.transpose(drawn_lists, (0, 2, 1, 3)).reshape(N_GRID * ATOM_DEV, LAYERS, SLOTS).astype(jnp.int32)


def block_scale(own_key, dims, shards, smallest, largest):
    gain, own = 1.0, jax.random.fold_in(own_key, 6)
    for axis_at, blocks in shards:
        steps = jnp.exp(jax.random.uniform(jax.random.fold_in(own, axis_at), (blocks,), jnp.float32, smallest / len(shards), largest / len(shards)))
        gain = gain * jnp.repeat(steps, dims[axis_at] // blocks).reshape([-1 if axis == axis_at else 1 for axis in range(len(dims))])
    return gain


def bell_draw(rng, extent, deviation, most, cuts=(), held_as=jnp.bfloat16):
    level = block_scale(rng, extent, cuts, -0.22, 0.18) if cuts else 1.0
    result = jax.random.normal(rng, extent, jnp.float32) * deviation * level
    return jnp.minimum(jnp.maximum(result, -most), most).astype(held_as)


def setup_inputs(seed: int = 0) -> dict:
    splits = jax.random.split(jax.random.key(seed), 5)
    support = bell_draw(splits[0], (ATOMS, FUNCS, BOX, BOX * BOX), 0.06, 0.359375, ((0, 8), (2, 4)))
    potential = bell_draw(splits[1], (BLOCKS, BLOCK ** 3), 1.0, 6.0, ((0, 32),))
    kernel = bell_draw(splits[2], (ATOMS, FUNCS, FUNCS), 3.0, 18.0, ((0, 8),), jnp.float32)
    block_list = draw_block_list(jax.random.fold_in(splits[4], 71), 0)
    return {"support": support, "potential": potential, "kernel": kernel, "block_list": block_list}


STENCIL_WEIGHTS = (-5369.0 / 1800.0, 12.0 / 7.0, -15.0 / 56.0, 10.0 / 189.0, -1.0 / 112.0, 2.0 / 1925.0, -1.0 / 16632.0)
CELL_VOLUME = 0.125
KINETIC_FACTOR = 2.0


def sphere_inside():
    coords = 2 * jnp.arange(BOX, dtype=jnp.int32) - (BOX - 1)
    squares = coords * coords
    summed = squares[:, None, None] + squares[None, :, None] + squares[None, None, :]
    return summed <= (2 * RADIUS) ** 2


def second_difference(values, direction):
    stencil_reach = len(STENCIL_WEIGHTS) - 1
    widths = [(0, 0)] * values.ndim
    widths[direction] = (stencil_reach, stencil_reach)
    padded = jnp.pad(values, widths)
    length = values.shape[direction]
    summed = STENCIL_WEIGHTS[0] * values
    for offset in range(1, stencil_reach + 1):
        forward = lax.slice_in_dim(padded, stencil_reach + offset, stencil_reach + offset + length, axis=direction)
        backward = lax.slice_in_dim(padded, stencil_reach - offset, stencil_reach - offset + length, axis=direction)
        summed = summed + STENCIL_WEIGHTS[offset] * (forward + backward)
    return summed


def reference(support, potential, kernel, block_list):
    inside = sphere_inside()

    def one_atom(operands):
        values, kernel_block, block_ids = operands
        masked = jnp.where(inside[None], values.reshape(FUNCS, BOX, BOX, BOX), jnp.zeros((), jnp.bfloat16))
        field_values = masked.astype(jnp.float32)
        blocks = jnp.take(potential, block_ids.reshape(-1), axis=0)
        blocks = blocks.reshape(LAYERS, SIDE_BLOCKS, SIDE_BLOCKS, BLOCK, BLOCK, BLOCK)
        potential_box = jnp.transpose(blocks, (0, 3, 1, 4, 2, 5)).reshape(BOX, BOX, BOX)
        laplace = (second_difference(field_values, 1) + second_difference(field_values, 2)) + second_difference(field_values, 3)
        applied_full = jnp.where(inside[None], -KINETIC_FACTOR * laplace + potential_box.astype(jnp.float32)[None] * field_values, 0.0)
        field_flat = field_values.reshape(FUNCS, -1)
        applied_flat = applied_full.reshape(FUNCS, -1)
        matrix_block = CELL_VOLUME * jnp.einsum("fp,gp->fg", field_flat, applied_flat, precision=lax.Precision.HIGHEST)
        mixed_field = jnp.einsum("fg,gp->fp", kernel_block, field_flat, precision=lax.Precision.HIGHEST)
        deposit = jnp.sum(field_flat * mixed_field, axis=0)
        deposit = deposit.reshape(LAYERS, BLOCK, SIDE_BLOCKS, BLOCK, SIDE_BLOCKS, BLOCK)
        deposit = jnp.transpose(deposit, (0, 2, 4, 1, 3, 5)).reshape(LAYERS * SLOTS, BLOCK ** 3)
        applied = applied_full.reshape(FUNCS, BOX, BOX * BOX).astype(jnp.bfloat16)
        return applied, matrix_block, deposit

    applied, hamiltonian, deposits = lax.map(one_atom, (support, kernel, block_list))
    density = jax.ops.segment_sum(deposits.reshape(-1, BLOCK ** 3), block_list.reshape(-1), num_segments=BLOCKS)
    return applied, density, hamiltonian
```

```python
import functools

import jax
import jax.numpy as jnp
import ml_dtypes
import numpy as np
from jax import lax
from jax.experimental import pallas as pl
from jax.experimental.pallas import tpu as pltpu
from jax.sharding import PartitionSpec as P

FUNCS = 4
BOX = 32
BLOCK = 8
RADIUS = 13
SIDE = 4
REACH = 6
TILE = 256
WEIGHTS = (
    -5369.0 / 1800.0,
    12.0 / 7.0,
    -15.0 / 56.0,
    10.0 / 189.0,
    -1.0 / 112.0,
    2.0 / 1925.0,
    -1.0 / 16632.0,
)
CELL_VOLUME = 0.125
KINETIC = -2.0
MESH = pl.DeviceIdType.MESH
F32 = jnp.float32
BF16 = jnp.bfloat16


def split(array):
    high = array.astype(ml_dtypes.bfloat16)
    low = (array - high.astype(np.float64)).astype(ml_dtypes.bfloat16)
    return high, low


def band(offset):
    weight = np.zeros(offset.shape)
    for k in range(1, REACH + 1):
        weight = np.where(np.abs(offset) == k, WEIGHTS[k], weight)
    return KINETIC * weight


def constants(rows):
    lane = np.arange(TILE)
    y, z = lane // BOX, lane % BOX
    parts = []
    for shift in (-BLOCK, 0, BLOCK):
        from_y = (y + shift)[:, None]
        matrix = band(y[None] - from_y) * (z[:, None] == z[None])
        if shift == 0:
            matrix = matrix + band(z[None] - z[:, None]) * (y[:, None] == y[None])
            matrix = matrix + 3 * KINETIC * WEIGHTS[0] * np.eye(TILE)
        parts.extend(split(matrix))
    plane = np.concatenate(parts, axis=0)

    row = np.arange(rows)
    pair, x = row // BLOCK, row % BLOCK
    halo = np.arange(rows // BLOCK * REACH)
    halo_pair, halo_x = halo // REACH, halo % REACH
    same = pair[:, None] == halo_pair[None]
    before = band(x[:, None] - (halo_x - REACH)[None]) * same
    after = band(x[:, None] - (halo_x + BLOCK)[None]) * same
    centre = band(x[:, None] - x[None]) * (pair[:, None] == pair[None])
    depth = np.concatenate(split(np.concatenate([centre, before, after], axis=1)), axis=0)

    up = (halo_x + BLOCK - REACH)[:, None] == x[None]
    down = halo_x[:, None] == x[None]
    select = np.concatenate([up & same.T, down & same.T], axis=0)

    spot = np.arange(128)
    half, cell = spot // 64, spot % 64
    match = (cell // 8)[:, None] == y[None]
    match = match & ((cell % 8)[:, None] == (z % 8)[None])
    spread = np.concatenate([match & (half == h)[:, None] for h in (0, 1)], axis=1)

    column = np.arange(SIDE * 128)
    slot, side, goal = column // 128, column % 128 // 64, column % 64
    here = (y[:, None] == (goal // 8)[None]) & (z[:, None] == (slot * 8 + goal % 8)[None])
    gather = np.concatenate([here & (side == h)[None] for h in (0, 1)], axis=0)

    to = ml_dtypes.bfloat16
    return plane, depth, select.astype(to), spread.astype(to), gather.astype(to)


def dot(a, b, dims=((1,), (0,)), precision=None):
    return lax.dot_general(
        a, b, (dims, ((), ())), precision=precision, preferred_element_type=F32
    )


def kernel_body(
    n, s, atoms, blocks,
    sup_hbm, pot, ker, bl, plane_hbm, depth_hbm, select_hbm, spread_hbm, gather_hbm,
    applied, density, ham,
    sup, plane, depth, select, spread, gather,
    field, fieldb, pre, halo_out, halo, pot_own, pot_all, dep_rows, dep_out, dep_in,
    ham_own, ham_all,
    load_sem, halo_send, halo_recv, pot_send, pot_recv, dep_send, dep_recv,
    ham_send, ham_recv,
):
    rows = atoms * FUNCS * BLOCK
    edge = rows // BLOCK * REACH
    part = blocks * 4
    me_g, me_s = lax.axis_index("grid"), lax.axis_index("slab")

    loads = [
        pltpu.make_async_copy(src, dst, load_sem.at[i])
        for i, (src, dst) in enumerate(
            (
                (sup_hbm, sup), (select_hbm, select), (gather_hbm, gather),
                (spread_hbm, spread), (plane_hbm, plane), (depth_hbm, depth),
            )
        )
    ]
    for load in loads:
        load.start()

    barrier = pltpu.get_barrier_semaphore()

    def greet(k, carry):
        pl.semaphore_signal(
            barrier, inc=1, device_id=(lax.rem(me_g + k, n), me_s), device_id_type=MESH
        )
        return carry

    lax.fori_loop(1, n, greet, 0)
    for k in range(1, s):
        pl.semaphore_signal(
            barrier, inc=1, device_id=(me_g, lax.rem(me_s + k, s)), device_id_type=MESH
        )

    own = pot[...].astype(F32)
    for c in range(4):
        dep_rows[c * blocks : (c + 1) * blocks, 0:128] = own[:, c * 128 : (c + 1) * 128]
    pot_own[...] = dep_rows[0:part, 0:128].astype(BF16)
    pot_all[pl.ds(me_g, 1)] = pot_own[...][None]

    x2 = 2 * (me_s * BLOCK + lax.broadcasted_iota(jnp.int32, (BLOCK, 1), 0)) - (BOX - 1)
    cells = lax.broadcasted_iota(jnp.int32, (1, BOX * BOX), 1)
    y2 = 2 * (cells // BOX) - (BOX - 1)
    z2 = 2 * (cells % BOX) - (BOX - 1)
    inside = (x2 * x2 + (y2 * y2 + z2 * z2)) <= (2 * RADIUS) ** 2
    loads[0].wait()
    for j in range(SIDE):
        lanes = slice(j * TILE, (j + 1) * TILE)
        values = sup[:, lanes].astype(F32).reshape(atoms * FUNCS, BLOCK, TILE)
        values = jnp.where(inside[None, :, lanes], values, 0.0).reshape(rows, TILE)
        field[:, lanes] = values
        fieldb[:, lanes] = values.astype(BF16)
    loads[1].wait()
    for j in range(SIDE):
        lanes = slice(j * TILE, (j + 1) * TILE)
        halo_out[j] = dot(select[...], fieldb[:, lanes]).astype(BF16)

    pl.semaphore_wait(barrier, n - 1 + s - 1)

    def pot_copy(k):
        return pltpu.make_async_remote_copy(
            src_ref=pot_own,
            dst_ref=pot_all.at[me_g],
            send_sem=pot_send,
            recv_sem=pot_recv,
            device_id=(lax.rem(me_g + k, n), me_s),
            device_id_type=MESH,
        )

    def send_pot(k, carry):
        pot_copy(k).start()
        return carry

    lax.fori_loop(1, n, send_pot, 0)

    def halo_copy(j, direction):
        first = direction * edge
        return pltpu.make_async_remote_copy(
            src_ref=halo_out.at[j, pl.ds(first, edge)],
            dst_ref=halo.at[j, pl.ds(first, edge)],
            send_sem=halo_send.at[direction, j],
            recv_sem=halo_recv.at[direction, j],
            device_id=(me_g, me_s + 1 - 2 * direction),
            device_id_type=MESH,
        )

    has_after, has_before = me_s < s - 1, me_s > 0

    @pl.when(has_after)
    def _():
        for j in range(SIDE):
            halo_copy(j, 0).start()

    @pl.when(has_before)
    def _():
        for j in range(SIDE):
            halo_copy(j, 1).start()

    @pl.when(jnp.logical_not(has_after))
    def _():
        halo[:, edge:, :] = jnp.zeros((SIDE, edge, TILE), BF16)

    @pl.when(jnp.logical_not(has_before))
    def _():
        halo[:, :edge, :] = jnp.zeros((SIDE, edge, TILE), BF16)

    for j in range(SIDE):
        lanes = slice(j * TILE, (j + 1) * TILE)
        for a in range(atoms):
            first = a * FUNCS * BLOCK
            f = [field[first + i * BLOCK : first + (i + 1) * BLOCK, lanes] for i in range(FUNCS)]
            total = None
            for i in range(FUNCS):
                mixed = ker[i, i, a] * f[i]
                for k in range(i + 1, FUNCS):
                    mixed = mixed + (ker[i, k, a] + ker[k, i, a]) * f[k]
                total = f[i] * mixed if total is None else total + f[i] * mixed
            at = (j * atoms + a) * BLOCK
            dep_rows[at : at + BLOCK, 0:TILE] = total
    dep = dep_rows[...]
    dep_high = dep.astype(BF16)
    dep_low = (dep - dep_high.astype(F32)).astype(BF16)
    loads[2].wait()
    sorted_dep = dot(jnp.concatenate([dep_high, dep_low], axis=1), gather[...]).astype(BF16)

    group = 8 if n % 8 == 0 else n
    span = group * part
    ids = bl[...]
    base = (lax.div(ids, s * blocks) * part + lax.rem(ids, blocks)).astype(F32)
    base = jnp.broadcast_to(base[:, None, :], (atoms, BLOCK, SIDE * SIDE))
    base = base.reshape(atoms * BLOCK, SIDE * SIDE)
    x = lax.broadcasted_iota(jnp.int32, (atoms * BLOCK, 1), 0) % BLOCK
    target = base + ((x % 2) * (n * part) + (x // 2) * blocks).astype(F32)
    index = lax.broadcasted_iota(jnp.int32, (1, 2 * span), 1)
    index = index // span * (n * part) + index % span

    def one_hot(first, zb):
        at = (index + first * part).astype(F32)
        return jnp.concatenate(
            [
                jnp.where(target[:, j * SIDE + zb : j * SIDE + zb + 1] == at, 1.0, 0.0).astype(BF16)
                for j in range(SIDE)
            ],
            axis=0,
        )

    low_half = lax.broadcasted_iota(jnp.int32, (1, 128), 1) < 64

    def deposit_group(g, carry):
        first = g * group
        total = jnp.zeros((2 * span, 128), F32)
        for zb in range(SIDE):
            total = total + dot(
                one_hot(first, zb), sorted_dep[:, zb * 128 : (zb + 1) * 128], ((0,), (0,))
            )
        total = total + pltpu.roll(total, 64, 1)
        dense = jnp.where(low_half, total[:span], total[span:])
        dep_out[pl.ds(first, group)] = dense.reshape(group, part, 128)
        return carry

    if n == group:
        deposit_group(0, 0)
    else:
        lax.fori_loop(0, n // group, deposit_group, 0)

    def send_dep(k, carry):
        peer = lax.rem(me_g + k, n)
        pltpu.make_async_remote_copy(
            src_ref=dep_out.at[peer],
            dst_ref=dep_in.at[k - 1],
            send_sem=dep_send,
            recv_sem=dep_recv,
            device_id=(peer, me_s),
            device_id_type=MESH,
        ).start()
        return carry

    lax.fori_loop(1, n, send_dep, 0)

    loads[4].wait()
    loads[5].wait()
    for j in range(SIDE):
        lanes = slice(j * TILE, (j + 1) * TILE)
        centre = dot(depth[:, 0:rows], fieldb[:, lanes])
        total = centre[:rows] + centre[rows:]
        for which, i in enumerate((j - 1, j, j + 1)):
            if 0 <= i < SIDE:
                f = fieldb[:, i * TILE : (i + 1) * TILE]
                at = which * 2 * TILE
                total = total + dot(f, plane[at : at + TILE, :])
                total = total + dot(f, plane[at + TILE : at + 2 * TILE, :])
        pre[:, lanes] = total

    loads[3].wait()
    pltpu.make_async_copy(
        pot_all.at[pl.ds(0, n - 1)], pot_all.at[pl.ds(0, n - 1)], pot_recv
    ).wait()
    zb_lane = lax.broadcasted_iota(jnp.int32, (1, TILE), 1) // BLOCK % SIDE

    def potential_group(g, total):
        first = g * group
        packed = pot_all[pl.ds(first, group)].reshape(span, 128)
        wide = dot(packed, spread[...]).astype(BF16)
        wide = jnp.concatenate([wide[:, 0:TILE], wide[:, TILE:]], axis=0)
        for zb in range(SIDE):
            found = dot(one_hot(first, zb), wide)
            total = jnp.where(zb_lane == zb, total + found, total)
        return total

    box = jnp.zeros((SIDE * atoms * BLOCK, TILE), F32)
    if n == group:
        box = potential_group(0, box)
    else:
        box = lax.fori_loop(0, n // group, potential_group, box)
    for j in range(SIDE):
        lanes = slice(j * TILE, (j + 1) * TILE)
        here = box[j * atoms * BLOCK : (j + 1) * atoms * BLOCK].reshape(atoms, 1, BLOCK, TILE)
        f = field[:, lanes].reshape(atoms, FUNCS, BLOCK, TILE)
        pre[:, lanes] = pre[:, lanes] + (here * f).reshape(rows, TILE)

    products = jnp.zeros((rows, rows), F32)
    for j in range(SIDE):
        lanes = slice(j * TILE, (j + 1) * TILE)

        @pl.when(has_before)
        def _():
            halo_copy(j, 0).wait_recv()

        @pl.when(has_after)
        def _():
            halo_copy(j, 1).wait_recv()

        outer = dot(depth[:, rows:], halo[j])
        full = pre[:, lanes] + outer[:rows] + outer[rows:]
        full = full.reshape(atoms * FUNCS, BLOCK, TILE)
        full = jnp.where(inside[None, :, lanes], full, 0.0).reshape(rows, TILE)
        high = full.astype(BF16)
        low = (full - high.astype(F32)).astype(BF16)
        applied[:, lanes] = high
        f = fieldb[:, lanes]
        products = products + dot(f, high, ((1,), (1,))) + dot(f, low, ((1,), (1,)))

    group_f = FUNCS * BLOCK
    ri = lax.broadcasted_iota(jnp.int32, (rows, rows), 0)
    ci = lax.broadcasted_iota(jnp.int32, (rows, rows), 1)
    keep = (ri // group_f == ci // group_f) & (ri % BLOCK == ci % BLOCK)
    products = jnp.where(keep, products, 0.0).reshape(atoms, FUNCS, BLOCK, rows)
    by_x = jnp.sum(products, axis=0)
    ham_own[0:FUNCS, :] = jnp.sum(by_x, axis=1)
    ham_own[FUNCS:, :] = jnp.zeros((8 - FUNCS, rows), F32)
    ham_all[pl.ds(me_s, 1)] = ham_own[...][None]
    ham_copies = [
        pltpu.make_async_remote_copy(
            src_ref=ham_own,
            dst_ref=ham_all.at[me_s],
            send_sem=ham_send.at[k],
            recv_sem=ham_recv.at[k],
            device_id=(me_g, lax.rem(me_s + k + 1, s)),
            device_id_type=MESH,
        )
        for k in range(s - 1)
    ]
    for copy in ham_copies:
        copy.start()

    pltpu.make_async_copy(dep_in, dep_in, dep_recv).wait()
    mine = lax.fori_loop(0, n - 1, lambda k, t: t + dep_in[k], dep_out[me_g])
    for c in range(4):
        density[:, c * 128 : (c + 1) * 128] = mine[c * blocks : (c + 1) * blocks]

    for copy in ham_copies:
        copy.wait_recv()
    whole = ham_all[0]
    for k in range(1, s):
        whole = whole + ham_all[k]
    ri = lax.broadcasted_iota(jnp.int32, (rows, FUNCS * 128), 0)
    ci = lax.broadcasted_iota(jnp.int32, (rows, FUNCS * 128), 1)
    fold = (ri // group_f == ci % 128) & (ri // BLOCK % FUNCS == ci // 128)
    whole = dot(whole, jnp.where(fold, CELL_VOLUME, 0.0), precision=lax.Precision.HIGHEST)
    for g in range(FUNCS):
        ham[:, g, :] = whole[0:FUNCS, g * 128 : g * 128 + atoms]

    for copy in ham_copies:
        copy.wait_send()
    pltpu.make_async_copy(
        pot_all.at[pl.ds(0, n - 1)], pot_all.at[pl.ds(0, n - 1)], pot_send
    ).wait()
    pltpu.make_async_copy(dep_in, dep_in, dep_send).wait()

    @pl.when(has_after)
    def _():
        for j in range(SIDE):
            halo_copy(j, 0).wait_send()

    @pl.when(has_before)
    def _():
        for j in range(SIDE):
            halo_copy(j, 1).wait_send()


def per_device(n, s, support, potential, kernel, block_list):
    atoms, _, _, cells = support.shape
    blocks = potential.shape[0]
    rows = atoms * FUNCS * BLOCK
    edge = rows // BLOCK * REACH
    part = blocks * 4
    consts = [jnp.asarray(c) for c in constants(rows)]
    vmem = pl.BlockSpec(memory_space=pltpu.VMEM)
    anywhere = pl.BlockSpec(memory_space=pl.ANY)
    dma = pltpu.SemaphoreType.DMA
    applied, density, ham = pl.pallas_call(
        functools.partial(kernel_body, n, s, atoms, blocks),
        out_shape=(
            jax.ShapeDtypeStruct((rows, cells), BF16),
            jax.ShapeDtypeStruct(potential.shape, F32),
            jax.ShapeDtypeStruct((FUNCS, FUNCS, atoms), F32),
        ),
        in_specs=[
            anywhere, vmem, pl.BlockSpec(memory_space=pltpu.SMEM), vmem,
            *([anywhere] * 5),
        ],
        out_specs=(vmem, vmem, vmem),
        scratch_shapes=[
            pltpu.VMEM((rows, cells), BF16),
            *[pltpu.VMEM(c.shape, BF16) for c in consts],
            pltpu.VMEM((rows, cells), F32),
            pltpu.VMEM((rows, cells), BF16),
            pltpu.VMEM((rows, cells), F32),
            pltpu.VMEM((SIDE, 2 * edge, TILE), BF16),
            pltpu.VMEM((SIDE, 2 * edge, TILE), BF16),
            pltpu.VMEM((part, 128), BF16),
            pltpu.VMEM((n, part, 128), BF16),
            pltpu.VMEM((SIDE * atoms * BLOCK, TILE), F32),
            pltpu.VMEM((n, part, 128), F32),
            pltpu.VMEM((n - 1, part, 128), F32),
            pltpu.VMEM((8, rows), F32),
            pltpu.VMEM((s, 8, rows), F32),
            dma((6,)), dma((2, SIDE)), dma((2, SIDE)), dma, dma, dma, dma,
            dma((s - 1,)), dma((s - 1,)),
        ],
        compiler_params=pltpu.CompilerParams(
            collective_id=0, has_side_effects=True, vmem_limit_bytes=48 * 1024 * 1024
        ),
    )(
        support.reshape(rows, cells),
        potential,
        jnp.transpose(kernel, (1, 2, 0)),
        block_list.reshape(atoms, -1),
        *consts,
    )
    return (
        applied.reshape(support.shape),
        density,
        jnp.transpose(ham, (2, 0, 1)),
    )


def solution(mesh):
    in_specs = (
        P("grid", None, "slab", None),
        P(("grid", "slab"), None),
        P("grid", None, None),
        P("grid", "slab", None),
    )
    out_specs = (P("grid", None, "slab", None), P(("grid", "slab"), None), P("grid", None, None))
    return jax.shard_map(
        functools.partial(per_device, mesh.shape["grid"], mesh.shape["slab"]),
        mesh=mesh, in_specs=in_specs, out_specs=out_specs, check_vma=False,
    )
```

```python
import functools

import jax
import jax.numpy as jnp
import ml_dtypes
import numpy as np
from jax import lax
from jax.experimental import pallas as pl
from jax.experimental.pallas import tpu as pltpu
from jax.sharding import PartitionSpec as P

FUNCS = 4
BOX = 32
BLOCK = 8
RADIUS = 13
SIDE = 4
REACH = 6
TILE = 256
WEIGHTS = (
    -5369.0 / 1800.0,
    12.0 / 7.0,
    -15.0 / 56.0,
    10.0 / 189.0,
    -1.0 / 112.0,
    2.0 / 1925.0,
    -1.0 / 16632.0,
)
CELL_VOLUME = 0.125
KINETIC = -2.0
MESH = pl.DeviceIdType.MESH
F32 = jnp.float32
BF16 = jnp.bfloat16


def split(array):
    high = array.astype(ml_dtypes.bfloat16)
    low = (array - high.astype(np.float64)).astype(ml_dtypes.bfloat16)
    return high, low


def band(offset):
    weight = np.zeros(offset.shape)
    for k in range(1, REACH + 1):
        weight = np.where(np.abs(offset) == k, WEIGHTS[k], weight)
    return KINETIC * weight


def constants(rows):
    lane = np.arange(TILE)
    y, z = lane // BOX, lane % BOX
    parts = []
    for shift in (-BLOCK, 0, BLOCK):
        from_y = (y + shift)[:, None]
        matrix = band(y[None] - from_y) * (z[:, None] == z[None])
        if shift == 0:
            matrix = matrix + band(z[None] - z[:, None]) * (y[:, None] == y[None])
            matrix = matrix + 3 * KINETIC * WEIGHTS[0] * np.eye(TILE)
        parts.extend(split(matrix))
    plane = np.concatenate(parts, axis=0)

    row = np.arange(rows)
    pair, x = row // BLOCK, row % BLOCK
    halo = np.arange(rows // BLOCK * REACH)
    halo_pair, halo_x = halo // REACH, halo % REACH
    same = pair[:, None] == halo_pair[None]
    before = band(x[:, None] - (halo_x - REACH)[None]) * same
    after = band(x[:, None] - (halo_x + BLOCK)[None]) * same
    centre = band(x[:, None] - x[None]) * (pair[:, None] == pair[None])
    depth = np.concatenate(split(np.concatenate([centre, before, after], axis=1)), axis=0)

    up = (halo_x + BLOCK - REACH)[:, None] == x[None]
    down = halo_x[:, None] == x[None]
    select = np.concatenate([up & same.T, down & same.T], axis=0)

    spot = np.arange(128)
    half, cell = spot // 64, spot % 64
    match = (cell // 8)[:, None] == y[None]
    match = match & ((cell % 8)[:, None] == (z % 8)[None])
    spread = np.concatenate([match & (half == h)[:, None] for h in (0, 1)], axis=1)

    column = np.arange(SIDE * 128)
    slot, side, goal = column // 128, column % 128 // 64, column % 64
    here = (y[:, None] == (goal // 8)[None]) & (z[:, None] == (slot * 8 + goal % 8)[None])
    gather = np.concatenate([here & (side == h)[None] for h in (0, 1)], axis=0)

    group = FUNCS * BLOCK
    keep = (row // group)[:, None] == (row // group)[None]
    keep = keep & (x[:, None] == x[None])
    lane = np.arange(128)
    fold = (row // group)[:, None] == (lane % 32)[None]
    fold = fold & ((pair % FUNCS)[:, None] == (lane // 32)[None])
    pick = np.concatenate([keep, CELL_VOLUME * fold], axis=1)

    to = ml_dtypes.bfloat16
    return plane, depth, *[c.astype(to) for c in (select, spread, gather, pick)]


def dot(a, b, dims=((1,), (0,)), precision=None):
    return lax.dot_general(
        a, b, (dims, ((), ())), precision=precision, preferred_element_type=F32
    )


def kernel_body(
    n, s, atoms, blocks,
    sup_hbm, pot_hbm, ker_hbm, bl_hbm, plane_hbm, depth_hbm, select_hbm, spread_hbm, gather_hbm, pick_hbm,
    applied_hbm, density_hbm, ham_all,
    sup, pot, ker, bl, plane, depth, select, spread, gather, pick,
    field, fieldb, pre, halo_out, halo, pot_own, pot_all, dep_rows, dep_out, dep_in,
    ham_own, chosen, applied, density,
    load_sem, store_sem, halo_send, halo_recv, pot_send, pot_recv, dep_send, dep_recv,
    ham_send, ham_recv,
):
    rows = atoms * FUNCS * BLOCK
    edge = rows // BLOCK * REACH
    part = blocks * 4
    me_g, me_s = lax.axis_index("grid"), lax.axis_index("slab")

    loads = [
        pltpu.make_async_copy(src, dst, load_sem.at[i])
        for i, (src, dst) in enumerate(
            (
                (sup_hbm, sup), (select_hbm, select), (gather_hbm, gather),
                (spread_hbm, spread), (plane_hbm, plane), (depth_hbm, depth),
                (pot_hbm, pot), (ker_hbm, ker), (bl_hbm, bl), (pick_hbm, pick),
            )
        )
    ]
    for i in (0, 6, 1, 7, 8, 2, 5, 4, 3, 9):
        loads[i].start()

    ham_own[...] = jnp.zeros(ham_own.shape, F32)
    barrier = pltpu.get_barrier_semaphore()

    def greet(k, carry):
        pl.semaphore_signal(
            barrier, inc=1, device_id=(lax.rem(me_g + k, n), me_s), device_id_type=MESH
        )
        return carry

    lax.fori_loop(1, n, greet, 0)
    for k in range(1, s):
        pl.semaphore_signal(
            barrier, inc=1, device_id=(me_g, lax.rem(me_s + k, s)), device_id_type=MESH
        )

    loads[6].wait()
    own = pot[...].astype(F32)
    for c in range(4):
        dep_rows[c * blocks : (c + 1) * blocks, 0:128] = own[:, c * 128 : (c + 1) * 128]
    pot_own[...] = dep_rows[0:part, 0:128].astype(BF16)
    pot_all[pl.ds(me_g, 1)] = pot_own[...][None]

    x2 = 2 * (me_s * BLOCK + lax.broadcasted_iota(jnp.int32, (BLOCK, 1), 0)) - (BOX - 1)
    cells = lax.broadcasted_iota(jnp.int32, (1, BOX * BOX), 1)
    y2 = 2 * (cells // BOX) - (BOX - 1)
    z2 = 2 * (cells % BOX) - (BOX - 1)
    inside = (x2 * x2 + (y2 * y2 + z2 * z2)) <= (2 * RADIUS) ** 2
    loads[0].wait()
    for j in range(SIDE):
        lanes = slice(j * TILE, (j + 1) * TILE)
        values = sup[:, lanes].astype(F32).reshape(atoms * FUNCS, BLOCK, TILE)
        values = jnp.where(inside[None, :, lanes], values, 0.0).reshape(rows, TILE)
        field[:, lanes] = values
        fieldb[:, lanes] = values.astype(BF16)
    loads[1].wait()
    for j in range(SIDE):
        lanes = slice(j * TILE, (j + 1) * TILE)
        halo_out[j] = dot(select[...], fieldb[:, lanes]).astype(BF16)

    pl.semaphore_wait(barrier, n - 1 + s - 1)

    def pot_copy(k):
        return pltpu.make_async_remote_copy(
            src_ref=pot_own,
            dst_ref=pot_all.at[me_g],
            send_sem=pot_send,
            recv_sem=pot_recv,
            device_id=(lax.rem(me_g + k, n), me_s),
            device_id_type=MESH,
        )

    def send_pot(k, carry):
        pot_copy(k).start()
        return carry


    def halo_copy(j, direction):
        first = direction * edge
        return pltpu.make_async_remote_copy(
            src_ref=halo_out.at[j, pl.ds(first, edge)],
            dst_ref=halo.at[j, pl.ds(first, edge)],
            send_sem=halo_send.at[direction, j],
            recv_sem=halo_recv.at[direction, j],
            device_id=(me_g, me_s + 1 - 2 * direction),
            device_id_type=MESH,
        )

    has_after, has_before = me_s < s - 1, me_s > 0

    @pl.when(has_after)
    def _():
        for j in range(SIDE):
            halo_copy(j, 0).start()

    @pl.when(has_before)
    def _():
        for j in range(SIDE):
            halo_copy(j, 1).start()

    lax.fori_loop(1, n, send_pot, 0)

    @pl.when(jnp.logical_not(has_after))
    def _():
        halo[:, edge:, :] = jnp.zeros((SIDE, edge, TILE), BF16)

    @pl.when(jnp.logical_not(has_before))
    def _():
        halo[:, :edge, :] = jnp.zeros((SIDE, edge, TILE), BF16)

    loads[7].wait()
    for j in range(SIDE):
        lanes = slice(j * TILE, (j + 1) * TILE)
        for a in range(atoms):
            first = a * FUNCS * BLOCK
            f = [field[first + i * BLOCK : first + (i + 1) * BLOCK, lanes] for i in range(FUNCS)]
            total = None
            for i in range(FUNCS):
                mixed = ker[i, i, a] * f[i]
                for k in range(i + 1, FUNCS):
                    mixed = mixed + (ker[i, k, a] + ker[k, i, a]) * f[k]
                total = f[i] * mixed if total is None else total + f[i] * mixed
            at = (j * atoms + a) * BLOCK
            dep_rows[at : at + BLOCK, 0:TILE] = total
    dep = dep_rows[...]
    dep_high = dep.astype(BF16)
    dep_low = (dep - dep_high.astype(F32)).astype(BF16)
    loads[2].wait()
    sorted_dep = dot(jnp.concatenate([dep_high, dep_low], axis=1), gather[...]).astype(BF16)

    group = 8 if n % 8 == 0 else n
    span = group * part
    loads[8].wait()
    ids = bl[...]
    base = (lax.div(ids, s * blocks) * part + lax.rem(ids, blocks)).astype(F32)
    base = jnp.broadcast_to(base[:, None, :], (atoms, BLOCK, SIDE * SIDE))
    base = base.reshape(atoms * BLOCK, SIDE * SIDE)
    x = lax.broadcasted_iota(jnp.int32, (atoms * BLOCK, 1), 0) % BLOCK
    target = base + ((x % 2) * (n * part) + (x // 2) * blocks).astype(F32)
    index = lax.broadcasted_iota(jnp.int32, (1, 2 * span), 1)
    index = index // span * (n * part) + index % span

    def one_hot(first, zb):
        at = (index + first * part).astype(F32)
        return jnp.concatenate(
            [
                jnp.where(target[:, j * SIDE + zb : j * SIDE + zb + 1] == at, 1.0, 0.0).astype(BF16)
                for j in range(SIDE)
            ],
            axis=0,
        )

    low_half = lax.broadcasted_iota(jnp.int32, (1, 128), 1) < 64

    if n == group:
        for zb in range(SIDE):
            chosen[zb] = one_hot(0, zb)

    def choice(first, zb):
        return chosen[zb] if n == group else one_hot(first, zb)

    def deposit_group(g, carry):
        first = g * group
        total = jnp.zeros((2 * span, 128), F32)
        for zb in range(SIDE):
            total = total + dot(
                choice(first, zb), sorted_dep[:, zb * 128 : (zb + 1) * 128], ((0,), (0,))
            )
        total = total + pltpu.roll(total, 64, 1)
        dense = jnp.where(low_half, total[:span], total[span:])
        dep_out[pl.ds(first, group)] = dense.reshape(group, part, 128)
        return carry

    if n == group:
        deposit_group(0, 0)
    else:
        lax.fori_loop(0, n // group, deposit_group, 0)

    def send_dep(k, carry):
        peer = lax.rem(me_g + k, n)
        pltpu.make_async_remote_copy(
            src_ref=dep_out.at[peer],
            dst_ref=dep_in.at[k - 1],
            send_sem=dep_send,
            recv_sem=dep_recv,
            device_id=(peer, me_s),
            device_id_type=MESH,
        ).start()
        return carry

    lax.fori_loop(1, n, send_dep, 0)

    loads[4].wait()
    loads[5].wait()
    for j in range(SIDE):
        lanes = slice(j * TILE, (j + 1) * TILE)
        centre = dot(depth[:, 0:rows], fieldb[:, lanes])
        total = centre[:rows] + centre[rows:]
        for which, i in enumerate((j - 1, j, j + 1)):
            if 0 <= i < SIDE:
                f = fieldb[:, i * TILE : (i + 1) * TILE]
                at = which * 2 * TILE
                total = total + dot(f, plane[at : at + TILE, :])
                total = total + dot(f, plane[at + TILE : at + 2 * TILE, :])
        pre[:, lanes] = total

    loads[3].wait()
    pltpu.make_async_copy(
        pot_all.at[pl.ds(0, n - 1)], pot_all.at[pl.ds(0, n - 1)], pot_recv
    ).wait()
    zb_lane = lax.broadcasted_iota(jnp.int32, (1, TILE), 1) // BLOCK % SIDE

    def potential_group(g, total):
        first = g * group
        packed = pot_all[pl.ds(first, group)].reshape(span, 128)
        wide = dot(packed, spread[...]).astype(BF16)
        wide = jnp.concatenate([wide[:, 0:TILE], wide[:, TILE:]], axis=0)
        for zb in range(SIDE):
            found = dot(choice(first, zb), wide)
            total = jnp.where(zb_lane == zb, total + found, total)
        return total

    box = jnp.zeros((SIDE * atoms * BLOCK, TILE), F32)
    if n == group:
        box = potential_group(0, box)
    else:
        box = lax.fori_loop(0, n // group, potential_group, box)
    for j in range(SIDE):
        lanes = slice(j * TILE, (j + 1) * TILE)
        here = box[j * atoms * BLOCK : (j + 1) * atoms * BLOCK].reshape(atoms, 1, BLOCK, TILE)
        f = field[:, lanes].reshape(atoms, FUNCS, BLOCK, TILE)
        pre[:, lanes] = pre[:, lanes] + (here * f).reshape(rows, TILE)

    products = jnp.zeros((rows, rows), F32)
    stores = []
    for j in range(SIDE):
        lanes = slice(j * TILE, (j + 1) * TILE)

        @pl.when(has_before)
        def _():
            halo_copy(j, 0).wait_recv()

        @pl.when(has_after)
        def _():
            halo_copy(j, 1).wait_recv()

        outer = dot(depth[:, rows:], halo[j])
        full = pre[:, lanes] + outer[:rows] + outer[rows:]
        full = full.reshape(atoms * FUNCS, BLOCK, TILE)
        full = jnp.where(inside[None, :, lanes], full, 0.0).reshape(rows, TILE)
        high = full.astype(BF16)
        low = (full - high.astype(F32)).astype(BF16)
        applied[:, lanes] = high
        stores.append(
            pltpu.make_async_copy(
                applied.at[:, pl.ds(j * TILE, TILE)],
                applied_hbm.at[:, pl.ds(j * TILE, TILE)],
                store_sem.at[j],
            )
        )
        stores[j].start()
        f = fieldb[:, lanes]
        products = products + dot(f, high, ((1,), (1,))) + dot(f, low, ((1,), (1,)))

    loads[9].wait()
    products = products * pick[:, 0:rows].astype(F32)
    products = jnp.sum(products.reshape(atoms, FUNCS, BLOCK, rows), axis=0)
    rest = jnp.sum(products, axis=1)
    terms = []
    for _ in range(3):
        terms.append(rest.astype(BF16).astype(F32))
        rest = rest - terms[-1]
    terms = jnp.concatenate(terms + [rest], axis=0).astype(BF16)
    folded = dot(terms, pick[:, rows:])
    ham_own[0:FUNCS, :] = (folded[8:12] + folded[4:8]) + folded[0:4]
    stores.append(pltpu.make_async_copy(ham_own, ham_all.at[me_s], store_sem.at[SIDE]))
    stores[SIDE].start()
    ham_copies = [
        pltpu.make_async_remote_copy(
            src_ref=ham_own,
            dst_ref=ham_all.at[me_s],
            send_sem=ham_send.at[k],
            recv_sem=ham_recv.at[k],
            device_id=(me_g, lax.rem(me_s + k + 1, s)),
            device_id_type=MESH,
        )
        for k in range(s - 1)
    ]
    for copy in ham_copies:
        copy.start()

    pltpu.make_async_copy(dep_in, dep_in, dep_recv).wait()
    mine = lax.fori_loop(0, n - 1, lambda k, t: t + dep_in[k], dep_out[me_g])
    for c in range(4):
        density[:, c * 128 : (c + 1) * 128] = mine[c * blocks : (c + 1) * blocks]
    stores.append(pltpu.make_async_copy(density, density_hbm, store_sem.at[SIDE + 1]))
    stores[SIDE + 1].start()

    for copy in ham_copies:
        copy.wait_recv()

    for copy in ham_copies:
        copy.wait_send()
    pltpu.make_async_copy(
        pot_all.at[pl.ds(0, n - 1)], pot_all.at[pl.ds(0, n - 1)], pot_send
    ).wait()
    pltpu.make_async_copy(dep_in, dep_in, dep_send).wait()

    @pl.when(has_after)
    def _():
        for j in range(SIDE):
            halo_copy(j, 0).wait_send()

    @pl.when(has_before)
    def _():
        for j in range(SIDE):
            halo_copy(j, 1).wait_send()

    for store in stores:
        store.wait()


def store_body(a, b, c, a_out, b_out, c_out, a_mid, b_mid, c_mid, ham, load_sem, store_sem):
    step = a.shape[0] // SIDE
    moves = [(c, c_mid, None), (b, b_mid, b_out)]
    for i in range(SIDE):
        at = pl.ds(i * step, step)
        moves.append((a.at[at], a_mid.at[at], a_out.at[at]))
    loads = [pltpu.make_async_copy(m[0], m[1], load_sem.at[i]) for i, m in enumerate(moves)]
    for load in loads:
        load.start()
    loads[0].wait()
    whole = c_mid[0]
    for k in range(1, c_mid.shape[0]):
        whole = whole + c_mid[k]
    for g in range(FUNCS):
        ham[:, g, :] = whole[0:FUNCS, g * 32 : g * 32 + ham.shape[2]]
    stores = [pltpu.make_async_copy(ham, c_out, store_sem.at[0])]
    stores[0].start()
    for i in range(1, SIDE + 2):
        loads[i].wait()
        stores.append(pltpu.make_async_copy(moves[i][1], moves[i][2], store_sem.at[i]))
        stores[i].start()
    for store in stores:
        store.wait()


def per_device(n, s, support, potential, kernel, block_list):
    atoms, _, _, cells = support.shape
    blocks = potential.shape[0]
    rows = atoms * FUNCS * BLOCK
    edge = rows // BLOCK * REACH
    part = blocks * 4
    consts = [jnp.asarray(c) for c in constants(rows)]
    hbm = pl.BlockSpec(memory_space=pltpu.HBM)
    dma = pltpu.SemaphoreType.DMA
    applied, density, ham = pl.pallas_call(
        functools.partial(kernel_body, n, s, atoms, blocks),
        out_shape=(
            jax.ShapeDtypeStruct((rows, cells), BF16),
            jax.ShapeDtypeStruct(potential.shape, F32),
            jax.ShapeDtypeStruct((s, 8, 128), F32),
        ),
        in_specs=[hbm] * 10,
        out_specs=(hbm, hbm, hbm),
        scratch_shapes=[
            pltpu.VMEM((rows, cells), BF16),
            pltpu.VMEM(potential.shape, BF16),
            pltpu.SMEM((FUNCS, FUNCS, atoms), F32),
            pltpu.VMEM((atoms, SIDE * SIDE), jnp.int32),
            *[pltpu.VMEM(c.shape, BF16) for c in consts],
            pltpu.VMEM((rows, cells), F32),
            pltpu.VMEM((rows, cells), BF16),
            pltpu.VMEM((rows, cells), F32),
            pltpu.VMEM((SIDE, 2 * edge, TILE), BF16),
            pltpu.VMEM((SIDE, 2 * edge, TILE), BF16),
            pltpu.VMEM((part, 128), BF16),
            pltpu.VMEM((n, part, 128), BF16),
            pltpu.VMEM((SIDE * atoms * BLOCK, TILE), F32),
            pltpu.VMEM((n, part, 128), F32),
            pltpu.VMEM((n - 1, part, 128), F32),
            pltpu.VMEM((8, 128), F32),
            pltpu.VMEM((SIDE, SIDE * atoms * BLOCK, 2 * min(n, 8) * part), BF16),
            pltpu.VMEM((rows, cells), BF16),
            pltpu.VMEM(potential.shape, F32),
            dma((10,)), dma((SIDE + 2,)), dma((2, SIDE)), dma((2, SIDE)), dma, dma, dma, dma,
            dma((s - 1,)), dma((s - 1,)),
        ],
        compiler_params=pltpu.CompilerParams(
            collective_id=0, has_side_effects=True, vmem_limit_bytes=64 * 1024 * 1024
        ),
    )(
        support.reshape(rows, cells),
        potential,
        jnp.transpose(kernel, (1, 2, 0)),
        block_list.reshape(atoms, -1),
        *consts,
    )
    results = (applied, density, ham)
    matrix = jax.ShapeDtypeStruct((FUNCS, FUNCS, atoms), F32)
    applied, density, ham = pl.pallas_call(
        store_body,
        out_shape=(
            jax.ShapeDtypeStruct((rows, cells), BF16),
            jax.ShapeDtypeStruct(potential.shape, F32),
            matrix,
        ),
        in_specs=[hbm] * 3,
        out_specs=(hbm,) * 3,
        scratch_shapes=[
            *[pltpu.VMEM(r.shape, r.dtype) for r in results],
            pltpu.VMEM(matrix.shape, F32),
            dma((SIDE + 2,)), dma((SIDE + 2,)),
        ],
        compiler_params=pltpu.CompilerParams(vmem_limit_bytes=64 * 1024 * 1024),
    )(*results)
    return (
        applied.reshape(support.shape),
        density,
        jnp.transpose(ham, (2, 0, 1)),
    )


def solution(mesh):
    in_specs = (
        P("grid", None, "slab", None),
        P(("grid", "slab"), None),
        P("grid", None, None),
        P("grid", "slab", None),
    )
    out_specs = (P("grid", None, "slab", None), P(("grid", "slab"), None), P("grid", None, None))
    return jax.shard_map(
        functools.partial(per_device, mesh.shape["grid"], mesh.shape["slab"]),
        mesh=mesh, in_specs=in_specs, out_specs=out_specs, check_vma=False,
    )
```

```python
import functools

import jax
import jax.numpy as jnp
import ml_dtypes
import numpy as np
from jax import lax
from jax.experimental import pallas as pl
from jax.experimental.pallas import tpu as pltpu
from jax.sharding import PartitionSpec as P

FUNCS = 4
BOX = 32
BLOCK = 8
RADIUS = 13
SIDE = 4
REACH = 6
WIDE = 2
TILE = 256
WEIGHTS = (
    -5369.0 / 1800.0,
    12.0 / 7.0,
    -15.0 / 56.0,
    10.0 / 189.0,
    -1.0 / 112.0,
    2.0 / 1925.0,
    -1.0 / 16632.0,
)
CELL_VOLUME = 0.125
KINETIC = -2.0
MESH = pl.DeviceIdType.MESH
F32 = jnp.float32
BF16 = jnp.bfloat16


def split(array):
    high = array.astype(ml_dtypes.bfloat16)
    low = (array - high.astype(np.float64)).astype(ml_dtypes.bfloat16)
    return high, low


def band(offset):
    weight = np.zeros(offset.shape)
    for k in range(1, REACH + 1):
        weight = np.where(np.abs(offset) == k, WEIGHTS[k], weight)
    return KINETIC * weight


def constants(rows):
    lane = np.arange(TILE)
    y, z = lane // BOX, lane % BOX
    parts = []
    for shift in (-BLOCK, 0, BLOCK):
        from_y = (y + shift)[:, None]
        matrix = band(y[None] - from_y) * (z[:, None] == z[None])
        if shift == 0:
            matrix = matrix + band(z[None] - z[:, None]) * (y[:, None] == y[None])
            matrix = matrix + 3 * KINETIC * WEIGHTS[0] * np.eye(TILE)
        parts.extend(split(matrix))
    plane = np.concatenate(parts, axis=0)

    row = np.arange(rows)
    pair, x = row // BLOCK, row % BLOCK
    halo = np.arange(rows // BLOCK * REACH)
    halo_pair, halo_x = halo // REACH, halo % REACH
    same = pair[:, None] == halo_pair[None]
    before = band(x[:, None] - (halo_x - REACH)[None]) * same
    after = band(x[:, None] - (halo_x + BLOCK)[None]) * same
    centre = band(x[:, None] - x[None]) * (pair[:, None] == pair[None])
    depth = np.concatenate(split(np.concatenate([centre, before, after], axis=1)), axis=0)

    up = (halo_x + BLOCK - REACH)[:, None] == x[None]
    down = halo_x[:, None] == x[None]
    select = np.concatenate([up & same.T, down & same.T], axis=0)

    spot = np.arange(128)
    half, cell = spot // 64, spot % 64
    match = (cell // 8)[:, None] == y[None]
    match = match & ((cell % 8)[:, None] == (z % 8)[None])
    spread = np.concatenate([match & (half == h)[:, None] for h in (0, 1)], axis=1)

    column = np.arange(SIDE * 128)
    slot, side, goal = column // 128, column % 128 // 64, column % 64
    here = (y[:, None] == (goal // 8)[None]) & (z[:, None] == (slot * 8 + goal % 8)[None])
    gather = np.concatenate([here & (side == h)[None] for h in (0, 1)], axis=0)

    group = FUNCS * BLOCK
    keep = (row // group)[:, None] == (row // group)[None]
    keep = keep & (x[:, None] == x[None])
    lane = np.arange(128)
    fold = (row // group)[:, None] == (lane % 32)[None]
    fold = fold & ((pair % FUNCS)[:, None] == (lane // 32)[None])
    pick = np.concatenate([keep, CELL_VOLUME * fold], axis=1)

    to = ml_dtypes.bfloat16
    return plane, depth, *[c.astype(to) for c in (select, spread, gather, pick)]


def dot(a, b, dims=((1,), (0,)), precision=None):
    return lax.dot_general(
        a, b, (dims, ((), ())), precision=precision, preferred_element_type=F32
    )


def kernel_body(
    n, s, atoms, blocks,
    sup_hbm, pot_hbm, ker_hbm, bl_hbm, plane_hbm, depth_hbm, select_hbm, spread_hbm, gather_hbm, pick_hbm,
    applied_hbm, density_hbm, ham_all,
    sup, pot, ker, bl, plane, depth, select, spread, gather, pick,
    field, fieldb, pre, halo_out, halo, pot_own, pot_all, dep_rows, dep_out, dep_in,
    ham_own, chosen, applied, density,
    load_sem, store_sem, halo_send, halo_recv, pot_send, pot_recv, dep_send, dep_recv,
    ham_send, ham_recv,
):
    rows = atoms * FUNCS * BLOCK
    edge = rows // BLOCK * REACH
    part = blocks * 4
    me_g, me_s = lax.axis_index("grid"), lax.axis_index("slab")

    loads = [
        pltpu.make_async_copy(src, dst, load_sem.at[i])
        for i, (src, dst) in enumerate(
            (
                (sup_hbm, sup), (select_hbm, select), (gather_hbm, gather),
                (spread_hbm, spread), (plane_hbm, plane), (depth_hbm, depth),
                (pot_hbm, pot), (ker_hbm, ker), (bl_hbm, bl), (pick_hbm, pick),
            )
        )
    ]
    for i in (0, 6, 1, 7, 8):
        loads[i].start()

    ham_own[...] = jnp.zeros(ham_own.shape, F32)
    barrier = pltpu.get_barrier_semaphore()

    def greet(k, carry):
        pl.semaphore_signal(
            barrier, inc=1, device_id=(lax.rem(me_g + k, n), me_s), device_id_type=MESH
        )
        return carry

    lax.fori_loop(1, n, greet, 0)
    for k in range(1, s):
        pl.semaphore_signal(
            barrier, inc=1, device_id=(me_g, lax.rem(me_s + k, s)), device_id_type=MESH
        )

    loads[6].wait()
    own = pot[...].astype(F32)
    for c in range(4):
        dep_rows[c * blocks : (c + 1) * blocks, 0:128] = own[:, c * 128 : (c + 1) * 128]
    pot_own[...] = dep_rows[0:part, 0:128].astype(BF16)
    pot_all[pl.ds(me_g, 1)] = pot_own[...][None]

    x2 = 2 * (me_s * BLOCK + lax.broadcasted_iota(jnp.int32, (BLOCK, 1), 0)) - (BOX - 1)
    cells = lax.broadcasted_iota(jnp.int32, (1, BOX * BOX), 1)
    y2 = 2 * (cells // BOX) - (BOX - 1)
    z2 = 2 * (cells % BOX) - (BOX - 1)
    inside = (x2 * x2 + (y2 * y2 + z2 * z2)) <= (2 * RADIUS) ** 2
    loads[0].wait()
    for j in range(SIDE):
        lanes = slice(j * TILE, (j + 1) * TILE)
        values = sup[:, lanes].astype(F32).reshape(atoms * FUNCS, BLOCK, TILE)
        values = jnp.where(inside[None, :, lanes], values, 0.0).reshape(rows, TILE)
        field[:, lanes] = values
        fieldb[:, lanes] = values.astype(BF16)
    for i in (2, 5, 4, 3, 9):
        loads[i].start()
    loads[1].wait()
    for j in range(SIDE):
        lanes = slice(j * TILE, (j + 1) * TILE)
        halo_out[j] = dot(select[...], fieldb[:, lanes]).astype(BF16)

    pl.semaphore_wait(barrier, n - 1 + s - 1)

    def pot_copy(k):
        return pltpu.make_async_remote_copy(
            src_ref=pot_own,
            dst_ref=pot_all.at[me_g],
            send_sem=pot_send,
            recv_sem=pot_recv,
            device_id=(lax.rem(me_g + k, n), me_s),
            device_id_type=MESH,
        )

    def send_pot(k, carry):
        pot_copy(k).start()
        return carry


    lax.fori_loop(1, n, send_pot, 0)

    def halo_copy(j, direction):
        first = direction * edge
        return pltpu.make_async_remote_copy(
            src_ref=halo_out.at[pl.ds(j * WIDE, WIDE), pl.ds(first, edge)],
            dst_ref=halo.at[pl.ds(j * WIDE, WIDE), pl.ds(first, edge)],
            send_sem=halo_send.at[direction, j],
            recv_sem=halo_recv.at[direction, j],
            device_id=(me_g, me_s + 1 - 2 * direction),
            device_id_type=MESH,
        )

    has_after, has_before = me_s < s - 1, me_s > 0

    @pl.when(has_after)
    def _():
        for j in range(SIDE // WIDE):
            halo_copy(j, 0).start()

    @pl.when(has_before)
    def _():
        for j in range(SIDE // WIDE):
            halo_copy(j, 1).start()

    @pl.when(jnp.logical_not(has_after))
    def _():
        halo[:, edge:, :] = jnp.zeros((SIDE, edge, TILE), BF16)

    @pl.when(jnp.logical_not(has_before))
    def _():
        halo[:, :edge, :] = jnp.zeros((SIDE, edge, TILE), BF16)

    loads[7].wait()
    for j in range(SIDE):
        lanes = slice(j * TILE, (j + 1) * TILE)
        for a in range(atoms):
            first = a * FUNCS * BLOCK
            f = [field[first + i * BLOCK : first + (i + 1) * BLOCK, lanes] for i in range(FUNCS)]
            total = None
            for i in range(FUNCS):
                mixed = ker[i, i, a] * f[i]
                for k in range(i + 1, FUNCS):
                    mixed = mixed + (ker[i, k, a] + ker[k, i, a]) * f[k]
                total = f[i] * mixed if total is None else total + f[i] * mixed
            at = (j * atoms + a) * BLOCK
            dep_rows[at : at + BLOCK, 0:TILE] = total
    dep = dep_rows[...]
    dep_high = dep.astype(BF16)
    dep_low = (dep - dep_high.astype(F32)).astype(BF16)
    loads[2].wait()
    sorted_dep = dot(jnp.concatenate([dep_high, dep_low], axis=1), gather[...]).astype(BF16)

    group = 8 if n % 8 == 0 else n
    span = group * part
    loads[8].wait()
    ids = bl[...]
    base = (lax.div(ids, s * blocks) * part + lax.rem(ids, blocks)).astype(F32)
    base = jnp.broadcast_to(base[:, None, :], (atoms, BLOCK, SIDE * SIDE))
    base = base.reshape(atoms * BLOCK, SIDE * SIDE)
    x = lax.broadcasted_iota(jnp.int32, (atoms * BLOCK, 1), 0) % BLOCK
    target = base + ((x % 2) * (n * part) + (x // 2) * blocks).astype(F32)
    index = lax.broadcasted_iota(jnp.int32, (1, 2 * span), 1)
    index = index // span * (n * part) + index % span

    def one_hot(first, zb):
        at = (index + first * part).astype(F32)
        return jnp.concatenate(
            [
                jnp.where(target[:, j * SIDE + zb : j * SIDE + zb + 1] == at, 1.0, 0.0).astype(BF16)
                for j in range(SIDE)
            ],
            axis=0,
        )

    low_half = lax.broadcasted_iota(jnp.int32, (1, 128), 1) < 64

    if n == group:
        for zb in range(SIDE):
            chosen[zb] = one_hot(0, zb)

    def choice(first, zb):
        return chosen[zb] if n == group else one_hot(first, zb)

    def deposit_group(g, carry):
        first = g * group
        total = jnp.zeros((2 * span, 128), F32)
        for zb in range(SIDE):
            total = total + dot(
                choice(first, zb), sorted_dep[:, zb * 128 : (zb + 1) * 128], ((0,), (0,))
            )
        total = total + pltpu.roll(total, 64, 1)
        dense = jnp.where(low_half, total[:span], total[span:])
        dep_out[pl.ds(first, group)] = dense.reshape(group, part, 128)
        return carry

    if n == group:
        deposit_group(0, 0)
    else:
        lax.fori_loop(0, n // group, deposit_group, 0)

    def send_dep(k, carry):
        peer = lax.rem(me_g + k, n)
        pltpu.make_async_remote_copy(
            src_ref=dep_out.at[peer],
            dst_ref=dep_in.at[k - 1],
            send_sem=dep_send,
            recv_sem=dep_recv,
            device_id=(peer, me_s),
            device_id_type=MESH,
        ).start()
        return carry

    lax.fori_loop(1, n, send_dep, 0)

    loads[4].wait()
    loads[5].wait()
    for j in range(SIDE):
        lanes = slice(j * TILE, (j + 1) * TILE)
        centre = dot(depth[:, 0:rows], fieldb[:, lanes])
        total = centre[:rows] + centre[rows:]
        for which, i in enumerate((j - 1, j, j + 1)):
            if 0 <= i < SIDE:
                f = fieldb[:, i * TILE : (i + 1) * TILE]
                at = which * 2 * TILE
                total = total + dot(f, plane[at : at + TILE, :])
                total = total + dot(f, plane[at + TILE : at + 2 * TILE, :])
        pre[:, lanes] = total

    loads[3].wait()
    pltpu.make_async_copy(
        pot_all.at[pl.ds(0, n - 1)], pot_all.at[pl.ds(0, n - 1)], pot_recv
    ).wait()
    zb_lane = lax.broadcasted_iota(jnp.int32, (1, TILE), 1) // BLOCK % SIDE

    def potential_group(g, total):
        first = g * group
        packed = pot_all[pl.ds(first, group)].reshape(span, 128)
        wide = dot(packed, spread[...]).astype(BF16)
        wide = jnp.concatenate([wide[:, 0:TILE], wide[:, TILE:]], axis=0)
        for zb in range(SIDE):
            found = dot(choice(first, zb), wide)
            total = jnp.where(zb_lane == zb, total + found, total)
        return total

    box = jnp.zeros((SIDE * atoms * BLOCK, TILE), F32)
    if n == group:
        box = potential_group(0, box)
    else:
        box = lax.fori_loop(0, n // group, potential_group, box)
    for j in range(SIDE):
        lanes = slice(j * TILE, (j + 1) * TILE)
        here = box[j * atoms * BLOCK : (j + 1) * atoms * BLOCK].reshape(atoms, 1, BLOCK, TILE)
        f = field[:, lanes].reshape(atoms, FUNCS, BLOCK, TILE)
        pre[:, lanes] = pre[:, lanes] + (here * f).reshape(rows, TILE)

    products = jnp.zeros((rows, rows), F32)
    stores = []
    for j in range(SIDE):
        lanes = slice(j * TILE, (j + 1) * TILE)

        if j % WIDE == 0:

            @pl.when(has_before)
            def _():
                halo_copy(j // WIDE, 0).wait_recv()

            @pl.when(has_after)
            def _():
                halo_copy(j // WIDE, 1).wait_recv()

        outer = dot(depth[:, rows:], halo[j])
        full = pre[:, lanes] + outer[:rows] + outer[rows:]
        full = full.reshape(atoms * FUNCS, BLOCK, TILE)
        full = jnp.where(inside[None, :, lanes], full, 0.0).reshape(rows, TILE)
        high = full.astype(BF16)
        low = (full - high.astype(F32)).astype(BF16)
        applied[:, lanes] = high
        stores.append(
            pltpu.make_async_copy(
                applied.at[:, pl.ds(j * TILE, TILE)],
                applied_hbm.at[:, pl.ds(j * TILE, TILE)],
                store_sem.at[j],
            )
        )
        stores[j].start()
        f = fieldb[:, lanes]
        products = products + dot(f, high, ((1,), (1,))) + dot(f, low, ((1,), (1,)))

    loads[9].wait()
    products = products * pick[:, 0:rows].astype(F32)
    products = jnp.sum(products.reshape(atoms, FUNCS, BLOCK, rows), axis=0)
    rest = jnp.sum(products, axis=1)
    terms = []
    for _ in range(3):
        terms.append(rest.astype(BF16).astype(F32))
        rest = rest - terms[-1]
    terms = jnp.concatenate(terms + [rest], axis=0).astype(BF16)
    folded = dot(terms, pick[:, rows:])
    ham_own[0:FUNCS, :] = (folded[8:12] + folded[4:8]) + folded[0:4]
    stores.append(pltpu.make_async_copy(ham_own, ham_all.at[me_s], store_sem.at[SIDE]))
    stores[SIDE].start()
    ham_copies = [
        pltpu.make_async_remote_copy(
            src_ref=ham_own,
            dst_ref=ham_all.at[me_s],
            send_sem=ham_send.at[k],
            recv_sem=ham_recv.at[k],
            device_id=(me_g, lax.rem(me_s + k + 1, s)),
            device_id_type=MESH,
        )
        for k in range(s - 1)
    ]
    for copy in ham_copies:
        copy.start()

    pltpu.make_async_copy(dep_in, dep_in, dep_recv).wait()
    mine = lax.fori_loop(0, n - 1, lambda k, t: t + dep_in[k], dep_out[me_g])
    for c in range(4):
        density[:, c * 128 : (c + 1) * 128] = mine[c * blocks : (c + 1) * blocks]
    stores.append(pltpu.make_async_copy(density, density_hbm, store_sem.at[SIDE + 1]))
    stores[SIDE + 1].start()

    for copy in ham_copies:
        copy.wait_recv()

    for copy in ham_copies:
        copy.wait_send()
    pltpu.make_async_copy(
        pot_all.at[pl.ds(0, n - 1)], pot_all.at[pl.ds(0, n - 1)], pot_send
    ).wait()
    pltpu.make_async_copy(dep_in, dep_in, dep_send).wait()

    @pl.when(has_after)
    def _():
        for j in range(SIDE // WIDE):
            halo_copy(j, 0).wait_send()

    @pl.when(has_before)
    def _():
        for j in range(SIDE // WIDE):
            halo_copy(j, 1).wait_send()

    for store in stores:
        store.wait()


def store_body(a, b, c, a_out, b_out, c_out, a_mid, b_mid, c_mid, ham, load_sem, store_sem):
    step = a.shape[0] // SIDE
    moves = [(c, c_mid, None), (b, b_mid, b_out)]
    for i in range(SIDE):
        at = pl.ds(i * step, step)
        moves.append((a.at[at], a_mid.at[at], a_out.at[at]))
    loads = [pltpu.make_async_copy(m[0], m[1], load_sem.at[i]) for i, m in enumerate(moves)]
    for load in loads:
        load.start()
    loads[0].wait()
    whole = c_mid[0]
    for k in range(1, c_mid.shape[0]):
        whole = whole + c_mid[k]
    for g in range(FUNCS):
        ham[:, g, :] = whole[0:FUNCS, g * 32 : g * 32 + ham.shape[2]]
    stores = [pltpu.make_async_copy(ham, c_out, store_sem.at[0])]
    stores[0].start()
    for i in range(1, SIDE + 2):
        loads[i].wait()
        stores.append(pltpu.make_async_copy(moves[i][1], moves[i][2], store_sem.at[i]))
        stores[i].start()
    for store in stores:
        store.wait()


def per_device(n, s, support, potential, kernel, block_list):
    atoms, _, _, cells = support.shape
    blocks = potential.shape[0]
    rows = atoms * FUNCS * BLOCK
    edge = rows // BLOCK * REACH
    part = blocks * 4
    consts = [jnp.asarray(c) for c in constants(rows)]
    hbm = pl.BlockSpec(memory_space=pltpu.HBM)
    dma = pltpu.SemaphoreType.DMA
    applied, density, ham = pl.pallas_call(
        functools.partial(kernel_body, n, s, atoms, blocks),
        out_shape=(
            jax.ShapeDtypeStruct((rows, cells), BF16),
            jax.ShapeDtypeStruct(potential.shape, F32),
            jax.ShapeDtypeStruct((s, 8, 128), F32),
        ),
        in_specs=[hbm] * 10,
        out_specs=(hbm, hbm, hbm),
        scratch_shapes=[
            pltpu.VMEM((rows, cells), BF16),
            pltpu.VMEM(potential.shape, BF16),
            pltpu.SMEM((FUNCS, FUNCS, atoms), F32),
            pltpu.VMEM((atoms, SIDE * SIDE), jnp.int32),
            *[pltpu.VMEM(c.shape, BF16) for c in consts],
            pltpu.VMEM((rows, cells), F32),
            pltpu.VMEM((rows, cells), BF16),
            pltpu.VMEM((rows, cells), F32),
            pltpu.VMEM((SIDE, 2 * edge, TILE), BF16),
            pltpu.VMEM((SIDE, 2 * edge, TILE), BF16),
            pltpu.VMEM((part, 128), BF16),
            pltpu.VMEM((n, part, 128), BF16),
            pltpu.VMEM((SIDE * atoms * BLOCK, TILE), F32),
            pltpu.VMEM((n, part, 128), F32),
            pltpu.VMEM((n - 1, part, 128), F32),
            pltpu.VMEM((8, 128), F32),
            pltpu.VMEM((SIDE, SIDE * atoms * BLOCK, 2 * min(n, 8) * part), BF16),
            pltpu.VMEM((rows, cells), BF16),
            pltpu.VMEM(potential.shape, F32),
            dma((10,)), dma((SIDE + 2,)), dma((2, SIDE)), dma((2, SIDE)), dma, dma, dma, dma,
            dma((s - 1,)), dma((s - 1,)),
        ],
        compiler_params=pltpu.CompilerParams(
            collective_id=0, has_side_effects=True, vmem_limit_bytes=64 * 1024 * 1024
        ),
    )(
        support.reshape(rows, cells),
        potential,
        jnp.transpose(kernel, (1, 2, 0)),
        block_list.reshape(atoms, -1),
        *consts,
    )
    results = (applied, density, ham)
    matrix = jax.ShapeDtypeStruct((FUNCS, FUNCS, atoms), F32)
    applied, density, ham = pl.pallas_call(
        store_body,
        out_shape=(
            jax.ShapeDtypeStruct((rows, cells), BF16),
            jax.ShapeDtypeStruct(potential.shape, F32),
            matrix,
        ),
        in_specs=[hbm] * 3,
        out_specs=(hbm,) * 3,
        scratch_shapes=[
            *[pltpu.VMEM(r.shape, r.dtype) for r in results],
            pltpu.VMEM(matrix.shape, F32),
            dma((SIDE + 2,)), dma((SIDE + 2,)),
        ],
        compiler_params=pltpu.CompilerParams(vmem_limit_bytes=64 * 1024 * 1024),
    )(*results)
    return (
        applied.reshape(support.shape),
        density,
        jnp.transpose(ham, (2, 0, 1)),
    )


def solution(mesh):
    in_specs = (
        P("grid", None, "slab", None),
        P(("grid", "slab"), None),
        P("grid", None, None),
        P("grid", "slab", None),
    )
    out_specs = (P("grid", None, "slab", None), P(("grid", "slab"), None), P("grid", None, None))
    return jax.shard_map(
        functools.partial(per_device, mesh.shape["grid"], mesh.shape["slab"]),
        mesh=mesh, in_specs=in_specs, out_specs=out_specs, check_vma=False,
    )
```

```python
import functools

import jax
import jax.numpy as jnp
import ml_dtypes
import numpy as np
from jax import lax
from jax.experimental import pallas as pl
from jax.experimental.pallas import tpu as pltpu
from jax.sharding import PartitionSpec as P

FUNCS = 4
BOX = 32
BLOCK = 8
RADIUS = 13
SIDE = 4
REACH = 6
WIDE = 2
TILE = 256
WEIGHTS = (
    -5369.0 / 1800.0,
    12.0 / 7.0,
    -15.0 / 56.0,
    10.0 / 189.0,
    -1.0 / 112.0,
    2.0 / 1925.0,
    -1.0 / 16632.0,
)
CELL_VOLUME = 0.125
KINETIC = -2.0
MESH = pl.DeviceIdType.MESH
F32 = jnp.float32
BF16 = jnp.bfloat16


def split(array):
    high = array.astype(ml_dtypes.bfloat16)
    low = (array - high.astype(np.float64)).astype(ml_dtypes.bfloat16)
    return high, low


def band(offset):
    weight = np.zeros(offset.shape)
    for k in range(1, REACH + 1):
        weight = np.where(np.abs(offset) == k, WEIGHTS[k], weight)
    return KINETIC * weight


def constants(rows):
    lane = np.arange(TILE)
    y, z = lane // BOX, lane % BOX
    parts = []
    for shift in (-BLOCK, 0, BLOCK):
        from_y = (y + shift)[:, None]
        matrix = band(y[None] - from_y) * (z[:, None] == z[None])
        if shift == 0:
            matrix = matrix + band(z[None] - z[:, None]) * (y[:, None] == y[None])
            matrix = matrix + 3 * KINETIC * WEIGHTS[0] * np.eye(TILE)
        parts.extend(split(matrix))
    plane = np.concatenate(parts, axis=0)

    row = np.arange(rows)
    pair, x = row // BLOCK, row % BLOCK
    halo = np.arange(rows // BLOCK * REACH)
    halo_pair, halo_x = halo // REACH, halo % REACH
    same = pair[:, None] == halo_pair[None]
    before = band(x[:, None] - (halo_x - REACH)[None]) * same
    after = band(x[:, None] - (halo_x + BLOCK)[None]) * same
    centre = band(x[:, None] - x[None]) * (pair[:, None] == pair[None])
    depth = np.concatenate(split(np.concatenate([centre, before, after], axis=1)), axis=0)

    up = (halo_x + BLOCK - REACH)[:, None] == x[None]
    down = halo_x[:, None] == x[None]
    select = np.concatenate([up & same.T, down & same.T], axis=0)

    spot = np.arange(128)
    half, cell = spot // 64, spot % 64
    match = (cell // 8)[:, None] == y[None]
    match = match & ((cell % 8)[:, None] == (z % 8)[None])
    spread = np.concatenate([match & (half == h)[:, None] for h in (0, 1)], axis=1)

    column = np.arange(SIDE * 128)
    slot, side, goal = column // 128, column % 128 // 64, column % 64
    here = (y[:, None] == (goal // 8)[None]) & (z[:, None] == (slot * 8 + goal % 8)[None])
    gather = np.concatenate([here & (side == h)[None] for h in (0, 1)], axis=0)

    group = FUNCS * BLOCK
    keep = (row // group)[:, None] == (row // group)[None]
    keep = keep & (x[:, None] == x[None])
    lane = np.arange(128)
    fold = (row // group)[:, None] == (lane % 32)[None]
    fold = fold & ((pair % FUNCS)[:, None] == (lane // 32)[None])
    pick = np.concatenate([keep, CELL_VOLUME * fold], axis=1)

    to = ml_dtypes.bfloat16
    return plane, depth, *[c.astype(to) for c in (select, spread, gather, pick)]


def dot(a, b, dims=((1,), (0,)), precision=None):
    return lax.dot_general(
        a, b, (dims, ((), ())), precision=precision, preferred_element_type=F32
    )


def kernel_body(
    n, s, atoms, blocks,
    sup_hbm, pot_hbm, ker_hbm, bl_hbm, plane_hbm, depth_hbm, select_hbm, spread_hbm, gather_hbm, pick_hbm,
    applied_hbm, density_hbm, ham_all,
    sup, pot, ker, bl, plane, depth, select, spread, gather, pick,
    field, fieldb, pre, halo_out, halo, pot_own, pot_all, dep_rows, dep_out, dep_in,
    ham_own, chosen, applied, density,
    load_sem, store_sem, halo_send, halo_recv, pot_send, pot_recv, dep_send, dep_recv,
    ham_send, ham_recv,
):
    rows = atoms * FUNCS * BLOCK
    edge = rows // BLOCK * REACH
    part = blocks * 4
    me_g, me_s = lax.axis_index("grid"), lax.axis_index("slab")

    loads = [
        pltpu.make_async_copy(src, dst, load_sem.at[i])
        for i, (src, dst) in enumerate(
            (
                (sup_hbm, sup), (select_hbm, select), (gather_hbm, gather),
                (spread_hbm, spread), (plane_hbm, plane), (depth_hbm, depth),
                (pot_hbm, pot), (ker_hbm, ker), (bl_hbm, bl), (pick_hbm, pick),
            )
        )
    ]
    for i in (0, 6, 1, 7, 8):
        loads[i].start()

    ham_own[...] = jnp.zeros(ham_own.shape, F32)
    barrier = pltpu.get_barrier_semaphore()

    def greet(k, carry):
        pl.semaphore_signal(
            barrier, inc=1, device_id=(lax.rem(me_g + k, n), me_s), device_id_type=MESH
        )
        return carry

    lax.fori_loop(1, n, greet, 0)
    for k in range(1, s):
        pl.semaphore_signal(
            barrier, inc=1, device_id=(me_g, lax.rem(me_s + k, s)), device_id_type=MESH
        )

    loads[6].wait()
    own = pot[...].astype(F32)
    for c in range(4):
        dep_rows[c * blocks : (c + 1) * blocks, 0:128] = own[:, c * 128 : (c + 1) * 128]
    pot_own[...] = dep_rows[0:part, 0:128].astype(BF16)
    pot_all[pl.ds(me_g, 1)] = pot_own[...][None]

    x2 = 2 * (me_s * BLOCK + lax.broadcasted_iota(jnp.int32, (BLOCK, 1), 0)) - (BOX - 1)
    cells = lax.broadcasted_iota(jnp.int32, (1, BOX * BOX), 1)
    y2 = 2 * (cells // BOX) - (BOX - 1)
    z2 = 2 * (cells % BOX) - (BOX - 1)
    inside = (x2 * x2 + (y2 * y2 + z2 * z2)) <= (2 * RADIUS) ** 2
    loads[0].wait()
    for j in range(SIDE):
        lanes = slice(j * TILE, (j + 1) * TILE)
        values = sup[:, lanes].astype(F32).reshape(atoms * FUNCS, BLOCK, TILE)
        values = jnp.where(inside[None, :, lanes], values, 0.0).reshape(rows, TILE)
        field[:, lanes] = values
        fieldb[:, lanes] = values.astype(BF16)
    for i in (2, 5, 4, 3, 9):
        loads[i].start()
    loads[1].wait()
    for j in range(SIDE):
        lanes = slice(j * TILE, (j + 1) * TILE)
        halo_out[j] = dot(select[...], fieldb[:, lanes]).astype(BF16)

    pl.semaphore_wait(barrier, n - 1 + s - 1)

    def pot_copy(k):
        return pltpu.make_async_remote_copy(
            src_ref=pot_own,
            dst_ref=pot_all.at[me_g],
            send_sem=pot_send,
            recv_sem=pot_recv,
            device_id=(lax.rem(me_g + k, n), me_s),
            device_id_type=MESH,
        )

    def send_pot(k, carry):
        pot_copy(k).start()
        return carry


    lax.fori_loop(1, n, send_pot, 0)

    def halo_copy(j, direction):
        first = direction * edge
        return pltpu.make_async_remote_copy(
            src_ref=halo_out.at[pl.ds(j * WIDE, WIDE), pl.ds(first, edge)],
            dst_ref=halo.at[pl.ds(j * WIDE, WIDE), pl.ds(first, edge)],
            send_sem=halo_send.at[direction, j],
            recv_sem=halo_recv.at[direction, j],
            device_id=(me_g, lax.rem(me_s + s + 1 - 2 * direction, s)),
            device_id_type=MESH,
        )

    has_after, has_before = me_s < s - 1, me_s > 0

    @pl.when(has_after)
    def _():
        for j in range(SIDE // WIDE):
            halo_copy(j, 0).start()

    @pl.when(has_before)
    def _():
        for j in range(SIDE // WIDE):
            halo_copy(j, 1).start()

    @pl.when(jnp.logical_not(has_after))
    def _():
        halo[:, edge:, :] = jnp.zeros((SIDE, edge, TILE), BF16)

    @pl.when(jnp.logical_not(has_before))
    def _():
        halo[:, :edge, :] = jnp.zeros((SIDE, edge, TILE), BF16)

    loads[7].wait()
    for j in range(SIDE):
        lanes = slice(j * TILE, (j + 1) * TILE)
        for a in range(atoms):
            first = a * FUNCS * BLOCK
            f = [field[first + i * BLOCK : first + (i + 1) * BLOCK, lanes] for i in range(FUNCS)]
            total = None
            for i in range(FUNCS):
                mixed = ker[i, i, a] * f[i]
                for k in range(i + 1, FUNCS):
                    mixed = mixed + (ker[i, k, a] + ker[k, i, a]) * f[k]
                total = f[i] * mixed if total is None else total + f[i] * mixed
            at = (j * atoms + a) * BLOCK
            dep_rows[at : at + BLOCK, 0:TILE] = total
    dep = dep_rows[...]
    dep_high = dep.astype(BF16)
    dep_low = (dep - dep_high.astype(F32)).astype(BF16)
    loads[2].wait()
    sorted_dep = dot(jnp.concatenate([dep_high, dep_low], axis=1), gather[...]).astype(BF16)

    group = 8 if n % 8 == 0 else n
    span = group * part
    loads[8].wait()
    ids = bl[...]
    base = (lax.div(ids, s * blocks) * part + lax.rem(ids, blocks)).astype(F32)
    base = jnp.broadcast_to(base[:, None, :], (atoms, BLOCK, SIDE * SIDE))
    base = base.reshape(atoms * BLOCK, SIDE * SIDE)
    x = lax.broadcasted_iota(jnp.int32, (atoms * BLOCK, 1), 0) % BLOCK
    target = base + ((x % 2) * (n * part) + (x // 2) * blocks).astype(F32)
    index = lax.broadcasted_iota(jnp.int32, (1, 2 * span), 1)
    index = index // span * (n * part) + index % span

    def one_hot(first, zb):
        at = (index + first * part).astype(F32)
        return jnp.concatenate(
            [
                jnp.where(target[:, j * SIDE + zb : j * SIDE + zb + 1] == at, 1.0, 0.0).astype(BF16)
                for j in range(SIDE)
            ],
            axis=0,
        )

    low_half = lax.broadcasted_iota(jnp.int32, (1, 128), 1) < 64

    if n == group:
        for zb in range(SIDE):
            chosen[zb] = one_hot(0, zb)

    def choice(first, zb):
        return chosen[zb] if n == group else one_hot(first, zb)

    def deposit_group(g, carry):
        first = g * group
        total = jnp.zeros((2 * span, 128), F32)
        for zb in range(SIDE):
            total = total + dot(
                choice(first, zb), sorted_dep[:, zb * 128 : (zb + 1) * 128], ((0,), (0,))
            )
        total = total + pltpu.roll(total, 64, 1)
        dense = jnp.where(low_half, total[:span], total[span:])
        dep_out[pl.ds(first, group)] = dense.reshape(group, part, 128)
        return carry

    if n == group:
        deposit_group(0, 0)
    else:
        lax.fori_loop(0, n // group, deposit_group, 0)

    def send_dep(k, carry):
        peer = lax.rem(me_g + k, n)
        pltpu.make_async_remote_copy(
            src_ref=dep_out.at[peer],
            dst_ref=dep_in.at[k - 1],
            send_sem=dep_send,
            recv_sem=dep_recv,
            device_id=(peer, me_s),
            device_id_type=MESH,
        ).start()
        return carry

    lax.fori_loop(1, n, send_dep, 0)

    loads[4].wait()
    loads[5].wait()
    for j in range(SIDE):
        lanes = slice(j * TILE, (j + 1) * TILE)
        centre = dot(depth[:, 0:rows], fieldb[:, lanes])
        total = centre[:rows] + centre[rows:]
        for which, i in enumerate((j - 1, j, j + 1)):
            if 0 <= i < SIDE:
                f = fieldb[:, i * TILE : (i + 1) * TILE]
                at = which * 2 * TILE
                total = total + dot(f, plane[at : at + TILE, :])
                total = total + dot(f, plane[at + TILE : at + 2 * TILE, :])
        pre[:, lanes] = total

    loads[3].wait()
    pltpu.make_async_copy(
        pot_all.at[pl.ds(0, n - 1)], pot_all.at[pl.ds(0, n - 1)], pot_recv
    ).wait()
    zb_lane = lax.broadcasted_iota(jnp.int32, (1, TILE), 1) // BLOCK % SIDE

    def potential_group(g, total):
        first = g * group
        packed = pot_all[pl.ds(first, group)].reshape(span, 128)
        wide = dot(packed, spread[...]).astype(BF16)
        wide = jnp.concatenate([wide[:, 0:TILE], wide[:, TILE:]], axis=0)
        for zb in range(SIDE):
            found = dot(choice(first, zb), wide)
            total = jnp.where(zb_lane == zb, total + found, total)
        return total

    box = jnp.zeros((SIDE * atoms * BLOCK, TILE), F32)
    if n == group:
        box = potential_group(0, box)
    else:
        box = lax.fori_loop(0, n // group, potential_group, box)
    for j in range(SIDE):
        lanes = slice(j * TILE, (j + 1) * TILE)
        here = box[j * atoms * BLOCK : (j + 1) * atoms * BLOCK].reshape(atoms, 1, BLOCK, TILE)
        f = field[:, lanes].reshape(atoms, FUNCS, BLOCK, TILE)
        pre[:, lanes] = pre[:, lanes] + (here * f).reshape(rows, TILE)

    products = jnp.zeros((rows, rows), F32)
    stores = []
    for j in range(SIDE):
        lanes = slice(j * TILE, (j + 1) * TILE)

        if j % WIDE == 0:

            @pl.when(has_before)
            def _():
                halo_copy(j // WIDE, 0).wait_recv()

            @pl.when(has_after)
            def _():
                halo_copy(j // WIDE, 1).wait_recv()

        outer = dot(depth[:, rows:], halo[j])
        full = pre[:, lanes] + outer[:rows] + outer[rows:]
        full = full.reshape(atoms * FUNCS, BLOCK, TILE)
        full = jnp.where(inside[None, :, lanes], full, 0.0).reshape(rows, TILE)
        high = full.astype(BF16)
        low = (full - high.astype(F32)).astype(BF16)
        applied[:, lanes] = high
        stores.append(
            pltpu.make_async_copy(
                applied.at[:, pl.ds(j * TILE, TILE)],
                applied_hbm.at[:, pl.ds(j * TILE, TILE)],
                store_sem.at[j],
            )
        )
        stores[j].start()
        f = fieldb[:, lanes]
        products = products + dot(f, high, ((1,), (1,))) + dot(f, low, ((1,), (1,)))

    loads[9].wait()
    products = products * pick[:, 0:rows].astype(F32)
    products = jnp.sum(products.reshape(atoms, FUNCS, BLOCK, rows), axis=0)
    rest = jnp.sum(products, axis=1)
    terms = []
    for _ in range(3):
        terms.append(rest.astype(BF16).astype(F32))
        rest = rest - terms[-1]
    terms = jnp.concatenate(terms + [rest], axis=0).astype(BF16)
    folded = dot(terms, pick[:, rows:])
    ham_own[0:FUNCS, :] = (folded[8:12] + folded[4:8]) + folded[0:4]
    stores.append(pltpu.make_async_copy(ham_own, ham_all.at[me_s], store_sem.at[SIDE]))
    stores[SIDE].start()
    ham_copies = [
        pltpu.make_async_remote_copy(
            src_ref=ham_own,
            dst_ref=ham_all.at[me_s],
            send_sem=ham_send.at[k],
            recv_sem=ham_recv.at[k],
            device_id=(me_g, lax.rem(me_s + k + 1, s)),
            device_id_type=MESH,
        )
        for k in range(s - 1)
    ]
    for copy in ham_copies:
        copy.start()

    pltpu.make_async_copy(dep_in, dep_in, dep_recv).wait()
    mine = lax.fori_loop(0, n - 1, lambda k, t: t + dep_in[k], dep_out[me_g])
    for c in range(4):
        density[:, c * 128 : (c + 1) * 128] = mine[c * blocks : (c + 1) * blocks]
    stores.append(pltpu.make_async_copy(density, density_hbm, store_sem.at[SIDE + 1]))
    stores[SIDE + 1].start()

    for copy in ham_copies:
        copy.wait_recv()

    for copy in ham_copies:
        copy.wait_send()
    pltpu.make_async_copy(
        pot_all.at[pl.ds(0, n - 1)], pot_all.at[pl.ds(0, n - 1)], pot_send
    ).wait()
    pltpu.make_async_copy(dep_in, dep_in, dep_send).wait()

    @pl.when(has_after)
    def _():
        for j in range(SIDE // WIDE):
            halo_copy(j, 0).wait_send()

    @pl.when(has_before)
    def _():
        for j in range(SIDE // WIDE):
            halo_copy(j, 1).wait_send()

    for store in stores:
        store.wait()


def store_body(a, b, c, a_out, b_out, c_out, a_mid, b_mid, c_mid, ham, load_sem, store_sem):
    step = a.shape[0] // SIDE
    moves = [(c, c_mid, None), (b, b_mid, b_out)]
    for i in range(SIDE):
        at = pl.ds(i * step, step)
        moves.append((a.at[at], a_mid.at[at], a_out.at[at]))
    loads = [pltpu.make_async_copy(m[0], m[1], load_sem.at[i]) for i, m in enumerate(moves)]
    for load in loads:
        load.start()
    loads[0].wait()
    whole = c_mid[0]
    for k in range(1, c_mid.shape[0]):
        whole = whole + c_mid[k]
    for g in range(FUNCS):
        ham[:, g, :] = whole[0:FUNCS, g * 32 : g * 32 + ham.shape[2]]
    stores = [pltpu.make_async_copy(ham, c_out, store_sem.at[0])]
    stores[0].start()
    for i in range(1, SIDE + 2):
        loads[i].wait()
        stores.append(pltpu.make_async_copy(moves[i][1], moves[i][2], store_sem.at[i]))
        stores[i].start()
    for store in stores:
        store.wait()


def per_device(n, s, support, potential, kernel, block_list):
    atoms, _, _, cells = support.shape
    blocks = potential.shape[0]
    rows = atoms * FUNCS * BLOCK
    edge = rows // BLOCK * REACH
    part = blocks * 4
    consts = [jnp.asarray(c) for c in constants(rows)]
    hbm = pl.BlockSpec(memory_space=pltpu.HBM)
    dma = pltpu.SemaphoreType.DMA
    applied, density, ham = pl.pallas_call(
        functools.partial(kernel_body, n, s, atoms, blocks),
        out_shape=(
            jax.ShapeDtypeStruct((rows, cells), BF16),
            jax.ShapeDtypeStruct(potential.shape, F32),
            jax.ShapeDtypeStruct((s, 8, 128), F32),
        ),
        in_specs=[hbm] * 10,
        out_specs=(hbm, hbm, hbm),
        scratch_shapes=[
            pltpu.VMEM((rows, cells), BF16),
            pltpu.VMEM(potential.shape, BF16),
            pltpu.SMEM((FUNCS, FUNCS, atoms), F32),
            pltpu.VMEM((atoms, SIDE * SIDE), jnp.int32),
            *[pltpu.VMEM(c.shape, BF16) for c in consts],
            pltpu.VMEM((rows, cells), F32),
            pltpu.VMEM((rows, cells), BF16),
            pltpu.VMEM((rows, cells), F32),
            pltpu.VMEM((SIDE, 2 * edge, TILE), BF16),
            pltpu.VMEM((SIDE, 2 * edge, TILE), BF16),
            pltpu.VMEM((part, 128), BF16),
            pltpu.VMEM((n, part, 128), BF16),
            pltpu.VMEM((SIDE * atoms * BLOCK, TILE), F32),
            pltpu.VMEM((n, part, 128), F32),
            pltpu.VMEM((n - 1, part, 128), F32),
            pltpu.VMEM((8, 128), F32),
            pltpu.VMEM((SIDE, SIDE * atoms * BLOCK, 2 * min(n, 8) * part), BF16),
            pltpu.VMEM((rows, cells), BF16),
            pltpu.VMEM(potential.shape, F32),
            dma((10,)), dma((SIDE + 2,)), dma((2, SIDE)), dma((2, SIDE)), dma, dma, dma, dma,
            dma((s - 1,)), dma((s - 1,)),
        ],
        compiler_params=pltpu.CompilerParams(
            collective_id=0, has_side_effects=True, vmem_limit_bytes=64 * 1024 * 1024
        ),
    )(
        support.reshape(rows, cells),
        potential,
        jnp.transpose(kernel, (1, 2, 0)),
        block_list.reshape(atoms, -1),
        *consts,
    )
    results = (applied, density, ham)
    matrix = jax.ShapeDtypeStruct((FUNCS, FUNCS, atoms), F32)
    applied, density, ham = pl.pallas_call(
        store_body,
        out_shape=(
            jax.ShapeDtypeStruct((rows, cells), BF16),
            jax.ShapeDtypeStruct(potential.shape, F32),
            matrix,
        ),
        in_specs=[hbm] * 3,
        out_specs=(hbm,) * 3,
        scratch_shapes=[
            *[pltpu.VMEM(r.shape, r.dtype) for r in results],
            pltpu.VMEM(matrix.shape, F32),
            dma((SIDE + 2,)), dma((SIDE + 2,)),
        ],
        compiler_params=pltpu.CompilerParams(vmem_limit_bytes=64 * 1024 * 1024),
    )(*results)
    return (
        applied.reshape(support.shape),
        density,
        jnp.transpose(ham, (2, 0, 1)),
    )


def solution(mesh):
    in_specs = (
        P("grid", None, "slab", None),
        P(("grid", "slab"), None),
        P("grid", None, None),
        P("grid", "slab", None),
    )
    out_specs = (P("grid", None, "slab", None), P(("grid", "slab"), None), P("grid", None, None))
    return jax.shard_map(
        functools.partial(per_device, mesh.shape["grid"], mesh.shape["slab"]),
        mesh=mesh, in_specs=in_specs, out_specs=out_specs, check_vma=False,
    )
```
